256 devices in a mesh: chan: 32 (over z, y_hi, core), seg: 4 (over x), win: 2 (over y_lo).
Axes of the slice: x: 4, y: 4 (y_hi: 2, y_lo: 2; y = y_hi * 2 + y_lo), z: 8, core: 2. Of those that a mesh axis runs over, the one named last changes fastest.
Arguments:
- series: bfloat16 [2048, 4096], P('chan', ('win', 'seg')), parts along dimension 1, may hold values from -200 to 200
Outputs:
- xcorr: bfloat16 [130, 2048, 2048], P('win', 'chan', 'seg'), parts along dimension 0
The draws below stay inside these ranges and needn't reach their ends.
There are 2 independent parts, one for each index of `win`. The reference program is written for one: setup_inputs(seed, part) draws one part's arguments, and reference() takes and returns one part's arrays. A program takes and returns all parts, laid end to end along the dimension named above; each array names one. Nothing has to cross between parts.
All inputs are finite; a program needn't handle non-finite values.
Results may differ from the reference program's by a relative error of at most 0.015.
Values may be sent and summed in bfloat16 or wider, within the bound.
No kernel may reach another device: no remote copies, remote signals or barrier semaphores. Data moves between devices by JAX's collectives and lax.ppermute only.
A program may use at most 128 MiB of HBM per device.

```python
import math
import jax
import jax.numpy as jnp
from jax import lax

HALF_LAG = 32
CHANNELS = 2048
SAMPLES = 2048
LAGS = 65


def draw_series(key, part):
    key = jax.random.fold_in(key, 11)
    key_amp, key_noise, key_wave, key_delay = jax.random.split(key, 4)
    amp = jnp.exp(jax.random.uniform(key_amp, (CHANNELS, 1), jnp.float32, 0.0, math.log(10.0)))
    noise = jax.random.normal(key_noise, (CHANNELS, SAMPLES), jnp.float32)
    weight = 0.6
    base = jax.random.normal(key_wave, (SAMPLES + 2 * HALF_LAG,), jnp.float32)
    delay = jax.random.randint(key_delay, (CHANNELS,), 0, 2 * HALF_LAG + 1)
    index = jnp.arange(SAMPLES, dtype=jnp.int32)[None, :] + delay[:, None]
    wave = base[index]
    envelope = jnp.exp(math.log(3.0) * jnp.arange(SAMPLES, dtype=jnp.float32) / SAMPLES)
    values = amp * envelope[None, :] * (noise + weight * wave)
    return jnp.clip(values, -200.0, 200.0).astype(jnp.bfloat16)


def setup_inputs(seed: int = 0, part: int = 0) -> dict:
    splits = jax.random.split(jax.random.key(seed), 2)
    own_keys = jax.random.split(jax.random.fold_in(splits[1], part), 2)
    return {
        "series": draw_series(jax.random.fold_in(jax.random.fold_in(splits[1], part), 71), part),
    }


def reference(series):
    values = series.astype(jnp.float32)
    energy = lax.optimization_barrier(jnp.sum(values * values, axis=1)) / SAMPLES + 1e-06
    scale = lax.rsqrt(energy)
    padded = jnp.pad(series, ((0, 0), (HALF_LAG, HALF_LAG)))

    def one_lag(index):
        shifted = lax.dynamic_slice_in_dim(padded, index, SAMPLES, 1)
        stacked = jnp.dot(series, shifted.T, preferred_element_type=jnp.float32)
        result = stacked * scale[:, None] * scale[None, :] / jnp.sqrt(jnp.float32(SAMPLES))
        return result.astype(jnp.bfloat16)
    return lax.map(one_lag, jnp.arange(LAGS, dtype=jnp.int32))
```

```python
import functools
import itertools

import jax
import jax.numpy as jnp
import numpy as np
from jax import lax
from jax.experimental import pallas as pl
from jax.experimental.pallas import tpu as pltpu
from jax.sharding import PartitionSpec as P

HALF_LAG = 32
LAGS = 2 * HALF_LAG + 1
AXES = ("chan", "seg", "win")
ZS, HS, KS, XS, WS = 8, 2, 2, 4, 2
EDGE = 128
GROUP = 5

DEST = np.array([0, 2, 6, 1, 5, 4, 5, 2, 7, 1, 7, 3, 6, 3, 0, 4, 4, 5, 3, 5, 3, 0, 1, 6, 1, 6, 4, 7, 2, 7, 2, 0, 7, 6, 2, 6, 0, 3, 1, 5, 2, 4, 0, 4, 1, 5, 7, 3, 3, 0, 5, 2, 4, 7, 6, 0, 6, 2, 3, 7, 5, 1, 4, 1, 1, 4, 3, 5, 3, 7, 2, 4, 6, 5, 1, 0, 2, 0, 6, 7, 0, 3, 0, 1, 4, 6, 7, 2, 5, 1, 4, 3, 7, 2, 5, 6, 5, 1, 4, 3, 6, 7, 6, 2, 0, 2, 5, 7, 4, 3, 0, 1, 7, 0, 7, 6, 1, 4, 2, 0, 2, 5, 3, 4, 3, 6, 1, 5]).reshape((4, 2, 4, 2, 2))
FROM = np.array([0, 1, 3, 3, 2, 2, 1, 0, 3, 0, 3, 1, 1, 3, 0, 2, 0, 1, 2, 3, 1, 0, 1, 0, 3, 2, 0, 1, 2, 3, 2, 2, 1, 0, 2, 1, 3, 3, 1, 3, 2, 2, 0, 0, 0, 1, 2, 3, 1, 2, 3, 2, 3, 3, 0, 1, 2, 0, 1, 0, 0, 1, 3, 2, 0, 3, 0, 2, 0, 2, 2, 0, 3, 3, 1, 1, 1, 0, 0, 2, 1, 0, 2, 1, 2, 2, 3, 0, 2, 1, 3, 3, 3, 1, 1, 3, 2, 0, 3, 1, 1, 0, 3, 3, 2, 2, 1, 1, 3, 3, 2, 0, 3, 1, 0, 2, 0, 2, 2, 3, 1, 3, 1, 0, 0, 1, 0, 2]).reshape((4, 8, 2, 2))
FIRST = np.array([0, 1, 1, 1, 1, 0, 0, 0, 0, 0, 0, 1, 1, 1, 1, 0, 1, 0, 0, 0, 1, 1, 0, 1, 0, 1, 1, 1, 0, 0, 0, 1]).reshape((4, 8))


def pairs(target):
    places = itertools.product(range(ZS), range(HS), range(KS), range(XS), range(WS))
    shape = (ZS, HS, KS, XS, WS)
    return [
        (int(np.ravel_multi_index(p, shape)), int(np.ravel_multi_index(target(*p), shape)))
        for p in places
    ]


def send(value, target):
    return lax.ppermute(value, AXES, pairs(target))


def along_x(step):
    return lambda z, h, k, x, w: (z, h, k, (x + step) % XS, w)


def other_y(z, h, k, x, w):
    return z, 1 - h, k, x, w


def other_core(z, h, k, x, w):
    return z, h, 1 - k, x, w


def to_columns(o):
    return lambda z, h, k, x, w: (int(DEST[z // 2, z % 2, x, k, o]), h, k, z // 2, w)


def stack_kernel(where, own, left, right, far, out, scale, rows):
    seg, samples = own.shape[1], own.shape[1] * XS
    x = where[0]

    @pl.when(pl.program_id(0) == 0)
    def _():
        rows[...] = jnp.zeros_like(rows)
        total = jnp.zeros((own.shape[0], 1), jnp.float32)
        for piece, step in ((own, 0), (left, XS - 1), (right, 1), (far, 2)):
            at = pl.multiple_of(EDGE + lax.rem(x + step, XS) * seg, EDGE)
            values = piece[...]
            rows[:, pl.ds(at, seg)] = values
            wide = values.astype(jnp.float32)
            total += jnp.sum(wide * wide, axis=1, keepdims=True)
        norm = lax.rsqrt(total / samples + 1e-06) * (1.0 / np.sqrt(samples))
        scale[...] = jnp.broadcast_to(norm, scale.shape)

    padded = rows[...]
    width = padded.shape[1]
    count = own.shape[0]
    for u in range(GROUP):
        lag = pl.program_id(0) * GROUP + u
        moved = pltpu.roll(padded, lag + (width - EDGE - HALF_LAG), 1)
        out[u * count : (u + 1) * count, :] = moved[:, :samples]


def lag_stack(where, own, left, right, far):
    count, seg = own.shape
    samples = seg * XS
    piece = pl.BlockSpec((count, seg), lambda g, s: (0, 0))
    return pl.pallas_call(
        stack_kernel,
        grid_spec=pltpu.PrefetchScalarGridSpec(
            num_scalar_prefetch=1,
            grid=(LAGS // GROUP,),
            in_specs=[piece] * 4,
            out_specs=[
                pl.BlockSpec((GROUP * count, samples), lambda g, s: (g, 0)),
                pl.BlockSpec((count, EDGE), lambda g, s: (0, 0)),
            ],
            scratch_shapes=[pltpu.VMEM((count, samples + 2 * EDGE), jnp.bfloat16)],
        ),
        out_shape=[
            jax.ShapeDtypeStruct((LAGS * count, samples), jnp.bfloat16),
            jax.ShapeDtypeStruct((count, EDGE), jnp.float32),
        ],
        compiler_params=pltpu.CompilerParams(vmem_limit_bytes=40 * 2**20),
    )(where, own, left, right, far)


def match_kernel(group, where, stack, row_scale, *refs):
    pieces, (out, columns, col_scale) = refs[:4], refs[-3:]
    count, seg = pieces[0].shape[1:]
    samples = seg * XS
    width = columns.shape[0]

    @pl.when(pl.program_id(0) == 0)
    def _():
        for n, piece in enumerate(pieces):
            row = pl.multiple_of(where[1 + n] * count, count)
            for q, step in enumerate((0, XS - 1, 1, 2)):
                at = pl.multiple_of(lax.rem(where[5 + n] + step, XS) * seg, EDGE)
                columns[pl.ds(row, count), pl.ds(at, seg)] = piece[q]
        wide = columns[...].astype(jnp.float32)
        total = jnp.sum(wide * wide, axis=1, keepdims=True)
        norm = lax.rsqrt(total / samples + 1e-06)
        col_scale[...] = jnp.broadcast_to(norm, (width, EDGE)).T[:8]

    products = lax.dot_general(
        stack[...], columns[...], (((1,), (1,)), ((), ())), preferred_element_type=jnp.float32
    )
    scaled = products.reshape(group, count, width) * row_scale[:, :1][None] * col_scale[:1][None]
    out[...] = scaled.astype(jnp.bfloat16)


def match(where, stack, row_scale, pieces, result, columns):
    count, seg = pieces[0].shape[1:]
    samples = seg * XS
    group = 13
    width = 4 * count
    whole = pl.BlockSpec(pieces[0].shape, lambda g, s: (0, 0, 0))
    before = [] if result is None else [result]
    return pl.pallas_call(
        functools.partial(match_kernel, group),
        grid_spec=pltpu.PrefetchScalarGridSpec(
            num_scalar_prefetch=1,
            grid=(LAGS // group,),
            in_specs=[
                pl.BlockSpec((group * count, samples), lambda g, s: (g, 0)),
                pl.BlockSpec((count, EDGE), lambda g, s: (0, 0)),
            ]
            + [whole] * 4
            + [pl.BlockSpec(memory_space=pl.ANY)] * len(before),
            out_specs=pl.BlockSpec((group, count, width), lambda g, s: (g, 0, s[0])),
            scratch_shapes=[
                pltpu.VMEM((width, samples), jnp.bfloat16),
                pltpu.VMEM((8, width), jnp.float32),
            ],
        ),
        out_shape=jax.ShapeDtypeStruct((LAGS, count, columns), jnp.bfloat16),
        input_output_aliases={7: 0} if before else {},
        compiler_params=pltpu.CompilerParams(vmem_limit_bytes=50 * 2**20),
        cost_estimate=pl.CostEstimate(
            flops=2 * LAGS * count * width * samples,
            bytes_accessed=2 * LAGS * count * (samples + width),
            transcendentals=0,
        ),
    )(where, stack, row_scale, *pieces, *before)


def on_device(series):
    count, seg = series.shape
    x = lax.axis_index("seg")
    chan = lax.axis_index("chan")
    z, h, k = chan // 4, chan // 2 % 2, chan % 2
    source = jnp.asarray(FROM, jnp.int32)[x, z]
    first = jnp.asarray(FIRST, jnp.int32)[x, z]

    left = send(series, along_x(1))
    right = send(series, along_x(-1))
    far = send(series, along_x(2))
    window = jnp.stack([series, left, right, far])
    stack, row_scale = lag_stack(jnp.stack([x]), series, left, right, far)

    result = None
    halves = []
    for o in range(2):
        mine = send(window, to_columns(o))
        beside = send(mine, other_y)
        halves.append((mine, beside, send(mine, other_core), send(beside, other_core)))
    for o, pieces in enumerate(halves):
        part = first if o == 0 else 1 - first
        places = [part]
        places += [h * 2 + k, (1 - h) * 2 + k, h * 2 + 1 - k, (1 - h) * 2 + 1 - k]
        places += [source[k, o], source[k, o], source[1 - k, o], source[1 - k, o]]
        where = jnp.stack([jnp.asarray(p, jnp.int32) for p in places])
        result = match(where, stack, row_scale, pieces, result, 8 * count)
    return result


def solution(mesh):
    placed = (P("chan", ("win", "seg")),)
    return jax.shard_map(
        on_device, mesh=mesh, in_specs=placed, out_specs=P("win", "chan", "seg"), check_vma=False
    )
```

```python
import functools
import itertools

import jax
import jax.numpy as jnp
import numpy as np
from jax import lax
from jax.experimental import pallas as pl
from jax.experimental.pallas import tpu as pltpu
from jax.sharding import PartitionSpec as P

HALF_LAG = 32
LAGS = 2 * HALF_LAG + 1
AXES = ("chan", "seg", "win")
ZS, HS, KS, XS, WS = 8, 2, 2, 4, 2
EDGE = 128

GROUP = 13
PHASES = 4
REACH = HALF_LAG // PHASES

DEST = np.array([0, 2, 6, 1, 5, 4, 5, 2, 7, 1, 7, 3, 6, 3, 0, 4, 4, 5, 3, 5, 3, 0, 1, 6, 1, 6, 4, 7, 2, 7, 2, 0, 7, 6, 2, 6, 0, 3, 1, 5, 2, 4, 0, 4, 1, 5, 7, 3, 3, 0, 5, 2, 4, 7, 6, 0, 6, 2, 3, 7, 5, 1, 4, 1, 1, 4, 3, 5, 3, 7, 2, 4, 6, 5, 1, 0, 2, 0, 6, 7, 0, 3, 0, 1, 4, 6, 7, 2, 5, 1, 4, 3, 7, 2, 5, 6, 5, 1, 4, 3, 6, 7, 6, 2, 0, 2, 5, 7, 4, 3, 0, 1, 7, 0, 7, 6, 1, 4, 2, 0, 2, 5, 3, 4, 3, 6, 1, 5]).reshape((4, 2, 4, 2, 2))
FIRST_BITS = -1900972002


def pairs(target):
    places = itertools.product(range(ZS), range(HS), range(KS), range(XS), range(WS))
    shape = (ZS, HS, KS, XS, WS)
    return [
        (int(np.ravel_multi_index(p, shape)), int(np.ravel_multi_index(target(*p), shape)))
        for p in places
    ]


def send(value, target):
    return lax.ppermute(value, AXES, pairs(target))


def along_x(step):
    return lambda z, h, k, x, w: (z, h, k, (x + step) % XS, w)


def other_y(z, h, k, x, w):
    return z, 1 - h, k, x, w


def other_core(z, h, k, x, w):
    return z, h, 1 - k, x, w


def to_columns(o):
    return lambda z, h, k, x, w: (int(DEST[z // 2, z % 2, x, k, o]), h, k, z // 2, w)


def part_of(me, o):
    bit = lax.rem(me, XS) * ZS + me // (XS * KS * HS)
    first = lax.shift_right_logical(jnp.int32(FIRST_BITS), bit.astype(jnp.int32)) & 1
    return first if o == 0 else 1 - first


def window_kernel(me, own, left, right, far, out):
    x = lax.rem(me[0], XS)
    seg = own.shape[1]
    sample = lax.broadcasted_iota(jnp.int32, (seg, seg), 0)
    place = lax.broadcasted_iota(jnp.int32, (seg, seg), 1)
    move = lax.rem(sample, PHASES) * EDGE + sample // PHASES == place
    move = jnp.where(move, 1.0, 0.0).astype(jnp.bfloat16)
    for piece, step in ((own, 0), (left, XS - 1), (right, 1), (far, 2)):
        values = jnp.dot(piece[...], move, preferred_element_type=jnp.float32)
        out[pl.ds(lax.rem(x + step, XS), 1)] = values.astype(jnp.bfloat16)[None]


def whole_window(me, own, left, right, far):
    return pl.pallas_call(
        window_kernel,
        in_specs=[pl.BlockSpec(memory_space=pltpu.SMEM)]
        + [pl.BlockSpec(memory_space=pltpu.VMEM)] * 4,
        out_specs=pl.BlockSpec(memory_space=pltpu.VMEM),
        out_shape=jax.ShapeDtypeStruct((XS,) + own.shape, own.dtype),
        compiler_params=pltpu.CompilerParams(vmem_limit_bytes=16 * 2**20),
    )(me, own, left, right, far)


def shift_kernel(window, out, scale):
    count, seg = window.shape[1:]
    edge = jnp.zeros((count, EDGE), jnp.bfloat16)
    total = jnp.zeros((count, 1), jnp.float32)
    for g in range(XS):
        wide = window[g].astype(jnp.float32)
        total += jnp.sum(wide * wide, axis=1, keepdims=True)
    samples = seg * XS
    norm = lax.rsqrt(total / samples + 1e-06) * (1.0 / np.sqrt(samples))
    scale[...] = jnp.broadcast_to(norm, scale.shape)
    for j in range(PHASES):
        tiles = [window[g, :, j * EDGE : (j + 1) * EDGE] for g in range(XS)]
        row = jnp.concatenate([edge] + tiles + [edge], axis=1)
        for o in range(2 * REACH + 1):
            moved = pltpu.roll(row, (REACH - o) % row.shape[1], 1)
            at = (PHASES * o + j) * EDGE
            for g in range(XS):
                out[g, :, at : at + EDGE] = moved[:, (g + 1) * EDGE : (g + 2) * EDGE]


def shifts(window):
    count, seg = window.shape[1:]
    width = (2 * REACH + 1) * PHASES * EDGE
    return pl.pallas_call(
        shift_kernel,
        in_specs=[pl.BlockSpec(memory_space=pltpu.VMEM)],
        out_specs=[pl.BlockSpec(memory_space=pltpu.VMEM)] * 2,
        out_shape=[
            jax.ShapeDtypeStruct((XS, count, width), jnp.bfloat16),
            jax.ShapeDtypeStruct((count, EDGE), jnp.float32),
        ],
        compiler_params=pltpu.CompilerParams(vmem_limit_bytes=16 * 2**20),
        cost_estimate=pl.CostEstimate(
            flops=0, bytes_accessed=8 * XS * count * width, transcendentals=0
        ),
    )(window)


def match_kernel(me, moved, row_scale, *refs):
    pieces, (out, columns, col_scale) = refs[:4], refs[-3:]
    count, seg = pieces[0].shape[1:]
    samples = seg * XS
    width = columns.shape[1]

    @pl.when(pl.program_id(0) == 0)
    def _():
        h, k = lax.rem(me[0] // (XS * KS), HS), lax.rem(me[0] // XS, KS)
        for piece, at in zip(pieces, (h * 2 + k, 2 - h * 2 + k, h * 2 + 1 - k, 3 - h * 2 - k)):
            row = pl.multiple_of(at * count, count)
            for g in range(XS):
                columns[g, pl.ds(row, count)] = piece[g]
        total = jnp.zeros((width, 1), jnp.float32)
        for g in range(XS):
            wide = columns[g].astype(jnp.float32)
            total += jnp.sum(wide * wide, axis=1, keepdims=True)
        norm = lax.rsqrt(total / samples + 1e-06)
        col_scale[...] = jnp.broadcast_to(norm, (width, EDGE)).T[:8]

    last = 2 * HALF_LAG - pl.program_id(0) * GROUP
    products = jnp.zeros((GROUP * count, width), jnp.float32)
    for g in range(XS):
        rows = jnp.concatenate(
            [
                moved[g, :, pl.ds(pl.multiple_of((last - u) * EDGE, EDGE), seg)]
                for u in range(GROUP)
            ],
            axis=0,
        )
        products += lax.dot_general(
            rows, columns[g], (((1,), (1,)), ((), ())), preferred_element_type=jnp.float32
        )
    scaled = products.reshape(GROUP, count, width) * row_scale[:, :1][None] * col_scale[:1][None]
    out[...] = scaled.astype(jnp.bfloat16)


def match(me, o, moved, row_scale, pieces, result, columns):
    count, seg = pieces[0].shape[1:]
    samples = seg * XS
    width = 4 * count
    inside = pl.BlockSpec(memory_space=pltpu.VMEM)
    before = [] if result is None else [result]
    return pl.pallas_call(
        match_kernel,
        grid_spec=pltpu.PrefetchScalarGridSpec(
            num_scalar_prefetch=1,
            grid=(LAGS // GROUP,),
            in_specs=[inside] * 6 + [pl.BlockSpec(memory_space=pl.ANY)] * len(before),
            out_specs=pl.BlockSpec((GROUP, count, width), lambda g, me: (g, 0, part_of(me[0], o))),
            scratch_shapes=[
                pltpu.VMEM((XS, width, seg), jnp.bfloat16),
                pltpu.VMEM((8, width), jnp.float32),
            ],
        ),
        out_shape=jax.ShapeDtypeStruct((LAGS, count, columns), jnp.bfloat16),
        input_output_aliases={7: 0} if before else {},
        compiler_params=pltpu.CompilerParams(vmem_limit_bytes=32 * 2**20),
        cost_estimate=pl.CostEstimate(
            flops=2 * LAGS * count * width * samples,
            bytes_accessed=2 * LAGS * count * width,
            transcendentals=0,
        ),
    )(me, moved, row_scale, *pieces, *before)


def on_device(series):
    count = series.shape[0]
    me = (lax.axis_index("chan") * XS + lax.axis_index("seg")).reshape(1)
    left = send(series, along_x(1))
    right = send(series, along_x(-1))
    far = send(series, along_x(2))
    window = whole_window(me, series, left, right, far)
    moved, row_scale = shifts(window)
    halves = []
    for o in range(2):
        mine = send(window, to_columns(o))
        beside = send(mine, other_y)
        halves.append((mine, beside, send(mine, other_core), send(beside, other_core)))
    result = None
    for o, pieces in enumerate(halves):
        result = match(me, o, moved, row_scale, pieces, result, 8 * count)
    return result


def solution(mesh):
    placed = (P("chan", ("win", "seg")),)
    return jax.shard_map(
        on_device, mesh=mesh, in_specs=placed, out_specs=P("win", "chan", "seg"), check_vma=False
    )
```

```python
import functools
import itertools

import jax
import jax.numpy as jnp
import numpy as np
from jax import lax
from jax.experimental import pallas as pl
from jax.experimental.pallas import tpu as pltpu
from jax.sharding import PartitionSpec as P

HALF_LAG = 32
LAGS = 2 * HALF_LAG + 1
AXES = ("chan", "seg", "win")
ZS, HS, KS, XS, WS = 8, 2, 2, 4, 2
EDGE = 128

GROUP = 13
PHASES = 4
REACH = HALF_LAG // PHASES

JUMP = ((2, 0, -2, 4), (-2, 4, 2, 0))


def pairs(target):
    places = itertools.product(range(ZS), range(HS), range(KS), range(XS), range(WS))
    shape = (ZS, HS, KS, XS, WS)
    return [
        (int(np.ravel_multi_index(p, shape)), int(np.ravel_multi_index(target(*p), shape)))
        for p in places
    ]


def send(value, target):
    return lax.ppermute(value, AXES, pairs(target))


def along_x(step):
    return lambda z, h, k, x, w: (z, h, k, (x + step) % XS, w)


def other_y(z, h, k, x, w):
    return z, 1 - h, k, x, w


def other_core(z, h, k, x, w):
    return z, h, 1 - k, x, w


def to_columns(z, h, k, x, w):
    jump = JUMP[k][x]
    return (z + jump) % ZS, h if jump % 4 == 0 else 1 - h, k, z // 2, w


def along_z(step):
    return lambda z, h, k, x, w: ((z + step) % ZS, h, k, x, w)


def held(me, step):
    h, z = lax.rem(me // (XS * KS), HS), me // (XS * KS * HS)
    q = (z - 2 * lax.rem(me, XS) + step) & 3
    return q & 1, h ^ (q >> 1)


def window_kernel(me, own, left, right, far, out):
    x = lax.rem(me[0], XS)
    seg = own.shape[1]
    sample = lax.broadcasted_iota(jnp.int32, (seg, seg), 0)
    place = lax.broadcasted_iota(jnp.int32, (seg, seg), 1)
    move = lax.rem(sample, PHASES) * EDGE + sample // PHASES == place
    move = jnp.where(move, 1.0, 0.0).astype(jnp.bfloat16)
    for piece, step in ((own, 0), (left, XS - 1), (right, 1), (far, 2)):
        values = jnp.dot(piece[...], move, preferred_element_type=jnp.float32)
        out[pl.ds(lax.rem(x + step, XS), 1)] = values.astype(jnp.bfloat16)[None]


def whole_window(me, own, left, right, far):
    return pl.pallas_call(
        window_kernel,
        in_specs=[pl.BlockSpec(memory_space=pltpu.SMEM)]
        + [pl.BlockSpec(memory_space=pltpu.VMEM)] * 4,
        out_specs=pl.BlockSpec(memory_space=pltpu.VMEM),
        out_shape=jax.ShapeDtypeStruct((XS,) + own.shape, own.dtype),
        compiler_params=pltpu.CompilerParams(vmem_limit_bytes=16 * 2**20),
    )(me, own, left, right, far)


def shift_kernel(window, out, scale):
    count, seg = window.shape[1:]
    edge = jnp.zeros((count, EDGE), jnp.bfloat16)
    total = jnp.zeros((count, 1), jnp.float32)
    for g in range(XS):
        wide = window[g].astype(jnp.float32)
        total += jnp.sum(wide * wide, axis=1, keepdims=True)
    samples = seg * XS
    norm = lax.rsqrt(total / samples + 1e-06) * (1.0 / np.sqrt(samples))
    scale[...] = jnp.broadcast_to(norm, scale.shape)
    for j in range(PHASES):
        tiles = [window[g, :, j * EDGE : (j + 1) * EDGE] for g in range(XS)]
        row = jnp.concatenate([edge] + tiles + [edge], axis=1)
        for o in range(2 * REACH + 1):
            moved = pltpu.roll(row, (REACH - o) % row.shape[1], 1)
            at = (PHASES * o + j) * EDGE
            for g in range(XS):
                out[g, :, at : at + EDGE] = moved[:, (g + 1) * EDGE : (g + 2) * EDGE]


def shifts(window):
    count, seg = window.shape[1:]
    width = (2 * REACH + 1) * PHASES * EDGE
    return pl.pallas_call(
        shift_kernel,
        in_specs=[pl.BlockSpec(memory_space=pltpu.VMEM)],
        out_specs=[pl.BlockSpec(memory_space=pltpu.VMEM)] * 2,
        out_shape=[
            jax.ShapeDtypeStruct((XS, count, width), jnp.bfloat16),
            jax.ShapeDtypeStruct((count, EDGE), jnp.float32),
        ],
        compiler_params=pltpu.CompilerParams(vmem_limit_bytes=16 * 2**20),
        cost_estimate=pl.CostEstimate(
            flops=0, bytes_accessed=8 * XS * count * width, transcendentals=0
        ),
    )(window)


def match_kernel(step, me, moved, row_scale, *refs):
    pieces, (out, columns, col_scale) = refs[:4], refs[-3:]
    count, seg = pieces[0].shape[1:]
    samples = seg * XS
    width = columns.shape[1]

    @pl.when(pl.program_id(0) == 0)
    def _():
        h, k = held(me[0], step)[1], lax.rem(me[0] // XS, KS)
        for piece, at in zip(pieces, (h * 2 + k, 2 - h * 2 + k, h * 2 + 1 - k, 3 - h * 2 - k)):
            row = pl.multiple_of(at * count, count)
            for g in range(XS):
                columns[g, pl.ds(row, count)] = piece[g]
        total = jnp.zeros((width, 1), jnp.float32)
        for g in range(XS):
            wide = columns[g].astype(jnp.float32)
            total += jnp.sum(wide * wide, axis=1, keepdims=True)
        norm = lax.rsqrt(total / samples + 1e-06)
        col_scale[...] = jnp.broadcast_to(norm, (width, EDGE)).T[:8]

    last = 2 * HALF_LAG - pl.program_id(0) * GROUP
    products = jnp.zeros((GROUP * count, width), jnp.float32)
    for g in range(XS):
        rows = jnp.concatenate(
            [
                moved[g, :, pl.ds(pl.multiple_of((last - u) * EDGE, EDGE), seg)]
                for u in range(GROUP)
            ],
            axis=0,
        )
        products += lax.dot_general(
            rows, columns[g], (((1,), (1,)), ((), ())), preferred_element_type=jnp.float32
        )
    scaled = products.reshape(GROUP, count, width) * row_scale[:, :1][None] * col_scale[:1][None]
    out[...] = scaled.astype(jnp.bfloat16)


def match(me, step, moved, row_scale, pieces, result, columns):
    count, seg = pieces[0].shape[1:]
    samples = seg * XS
    width = 4 * count
    inside = pl.BlockSpec(memory_space=pltpu.VMEM)
    before = [] if result is None else [result]
    return pl.pallas_call(
        functools.partial(match_kernel, step),
        grid_spec=pltpu.PrefetchScalarGridSpec(
            num_scalar_prefetch=1,
            grid=(LAGS // GROUP,),
            in_specs=[inside] * 6 + [pl.BlockSpec(memory_space=pl.ANY)] * len(before),
            out_specs=pl.BlockSpec((GROUP, count, width), lambda g, me: (g, 0, held(me[0], step)[0])),
            scratch_shapes=[
                pltpu.VMEM((XS, width, seg), jnp.bfloat16),
                pltpu.VMEM((8, width), jnp.float32),
            ],
        ),
        out_shape=jax.ShapeDtypeStruct((LAGS, count, columns), jnp.bfloat16),
        input_output_aliases={7: 0} if before else {},
        compiler_params=pltpu.CompilerParams(vmem_limit_bytes=32 * 2**20),
        cost_estimate=pl.CostEstimate(
            flops=2 * LAGS * count * width * samples,
            bytes_accessed=2 * LAGS * count * width,
            transcendentals=0,
        ),
    )(me, moved, row_scale, *pieces, *before)


def on_device(series):
    count = series.shape[0]
    me = (lax.axis_index("chan") * XS + lax.axis_index("seg")).reshape(1)
    left = send(series, along_x(1))
    right = send(series, along_x(-1))
    far = send(series, along_x(2))
    window = whole_window(me, series, left, right, far)
    moved, row_scale = shifts(window)
    mine = send(window, to_columns)
    mine, moved, row_scale = lax.optimization_barrier((mine, moved, row_scale))
    beside = send(mine, other_y)
    above = send(mine, along_z(-1))
    below = send(mine, along_z(1))
    result = None
    for step, (first, second) in enumerate(((mine, beside), (above, below))):
        pieces = (first, second, send(first, other_core), send(second, other_core))
        result = match(me, step, moved, row_scale, pieces, result, 8 * count)
    return result


def solution(mesh):
    placed = (P("chan", ("win", "seg")),)
    return jax.shard_map(
        on_device, mesh=mesh, in_specs=placed, out_specs=P("win", "chan", "seg"), check_vma=False
    )
```

```python
import functools
import itertools

import jax
import jax.numpy as jnp
import numpy as np
from jax import lax
from jax.experimental import pallas as pl
from jax.experimental.pallas import tpu as pltpu
from jax.sharding import PartitionSpec as P

HALF_LAG = 32
LAGS = 2 * HALF_LAG + 1
AXES = ("chan", "seg", "win")
ZS, HS, KS, XS, WS = 8, 2, 2, 4, 2
EDGE = 128

GROUP = 13
PHASES = 4
REACH = HALF_LAG // PHASES
PAIR = XS // 2
INSIDE = pl.BlockSpec(memory_space=pltpu.VMEM)

JUMP = ((2, 0, -2, 4), (-2, 4, 2, 0))


def pairs(target):
    places = itertools.product(range(ZS), range(HS), range(KS), range(XS), range(WS))
    shape = (ZS, HS, KS, XS, WS)
    return [
        (int(np.ravel_multi_index(p, shape)), int(np.ravel_multi_index(target(*p), shape)))
        for p in places
    ]


def send(value, target):
    return lax.ppermute(value, AXES, pairs(target))


def along_x(step):
    return lambda z, h, k, x, w: (z, h, k, (x + step) % XS, w)


def other_y(z, h, k, x, w):
    return z, 1 - h, k, x, w


def other_core(z, h, k, x, w):
    return z, h, 1 - k, x, w


def to_columns(z, h, k, x, w):
    jump = JUMP[k][x]
    return (z + jump) % ZS, h if jump % 4 == 0 else 1 - h, k, z // 2, w


def along_z(step):
    return lambda z, h, k, x, w: ((z + step) % ZS, h, k, x, w)


def held(me, step):
    h, z = lax.rem(me // (XS * KS), HS), me // (XS * KS * HS)
    q = (z - 2 * lax.rem(me, XS) + step) & 3
    return q & 1, h ^ (q >> 1)


def window_kernel(me, own, left, right, far, early, late):
    x = lax.rem(me[0], XS)
    seg = own.shape[1]
    sample = lax.broadcasted_iota(jnp.int32, (seg, seg), 0)
    place = lax.broadcasted_iota(jnp.int32, (seg, seg), 1)
    move = lax.rem(sample, PHASES) * EDGE + sample // PHASES == place
    move = jnp.where(move, 1.0, 0.0).astype(jnp.bfloat16)
    for piece, step in ((own, 0), (left, XS - 1), (right, 1), (far, 2)):
        values = jnp.dot(piece[...], move, preferred_element_type=jnp.float32)
        values = values.astype(jnp.bfloat16)[None]
        g = lax.rem(x + step, XS)

        @pl.when(g < PAIR)
        def _():
            early[pl.ds(g, 1)] = values

        @pl.when(g >= PAIR)
        def _():
            late[pl.ds(g - PAIR, 1)] = values


def whole_window(me, own, left, right, far):
    return pl.pallas_call(
        window_kernel,
        in_specs=[pl.BlockSpec(memory_space=pltpu.SMEM)] + [INSIDE] * 4,
        out_specs=[INSIDE] * 2,
        out_shape=[jax.ShapeDtypeStruct((PAIR,) + own.shape, own.dtype)] * 2,
        compiler_params=pltpu.CompilerParams(vmem_limit_bytes=16 * 2**20),
    )(me, own, left, right, far)


def shift_kernel(early, late, out, scale):
    count, seg = early.shape[1:]
    window = [early.at[0], early.at[1], late.at[0], late.at[1]]
    edge = jnp.zeros((count, EDGE), jnp.bfloat16)
    total = jnp.zeros((count, 1), jnp.float32)
    for g in range(XS):
        wide = window[g][...].astype(jnp.float32)
        total += jnp.sum(wide * wide, axis=1, keepdims=True)
    samples = seg * XS
    norm = lax.rsqrt(total / samples + 1e-06) * (1.0 / np.sqrt(samples))
    scale[...] = jnp.broadcast_to(norm, scale.shape)
    for j in range(PHASES):
        tiles = [window[g][:, j * EDGE : (j + 1) * EDGE] for g in range(XS)]
        row = jnp.concatenate([edge] + tiles + [edge], axis=1)
        for o in range(2 * REACH + 1):
            moved = pltpu.roll(row, (REACH - o) % row.shape[1], 1)
            at = (PHASES * o + j) * EDGE
            for g in range(XS):
                out[g, :, at : at + EDGE] = moved[:, (g + 1) * EDGE : (g + 2) * EDGE]


def shifts(early, late):
    count, seg = early.shape[1:]
    width = (2 * REACH + 1) * PHASES * EDGE
    return pl.pallas_call(
        shift_kernel,
        in_specs=[INSIDE] * 2,
        out_specs=[INSIDE] * 2,
        out_shape=[
            jax.ShapeDtypeStruct((XS, count, width), jnp.bfloat16),
            jax.ShapeDtypeStruct((count, EDGE), jnp.float32),
        ],
        compiler_params=pltpu.CompilerParams(vmem_limit_bytes=16 * 2**20),
        cost_estimate=pl.CostEstimate(
            flops=0, bytes_accessed=8 * XS * count * width, transcendentals=0
        ),
    )(early, late)


def place_columns(me, pieces, columns):
    count, seg = pieces[0].shape[1:]
    k = lax.rem(me // XS, KS)
    r, h = held(me, 0)
    r_up, h_up = held(me, 1)
    blocks = (r * 2 + h, r * 2 + 1 - h, r_up * 2 + h_up, r_up * 2 + 1 - h_up)
    for n, piece in enumerate(pieces):
        core = k if n < 4 else 1 - k
        row = pl.multiple_of((blocks[n % 4] * 2 + core) * count, count)
        for g in range(PAIR):
            columns[pl.ds(row, count), g * seg : (g + 1) * seg] = piece[g]
    wide = columns[...].astype(jnp.float32)
    total = jnp.sum(wide * wide, axis=1, keepdims=True)
    return jnp.broadcast_to(total, (columns.shape[0], EDGE)).T[:8]


def group_products(moved, columns, first_seg, group):
    seg = columns.shape[1] // PAIR
    last = 2 * HALF_LAG - group * GROUP
    rows = [
        [
            moved[first_seg + g, :, pl.ds(pl.multiple_of((last - u) * EDGE, EDGE), seg)]
            for g in range(PAIR)
        ]
        for u in range(GROUP)
    ]
    rows = jnp.concatenate([jnp.concatenate(row, axis=1) for row in rows], axis=0)
    products = lax.dot_general(
        rows, columns[...], (((1,), (1,)), ((), ())), preferred_element_type=jnp.float32
    )
    return products.reshape(GROUP, rows.shape[0] // GROUP, columns.shape[0])


def early_kernel(me, moved, *refs):
    pieces, (out, energy, columns) = refs[:8], refs[8:]
    energy[...] = place_columns(me[0], pieces, columns)
    for group in range(LAGS // GROUP):
        out[group * GROUP : (group + 1) * GROUP] = group_products(moved, columns, 0, group)


def match_early(me, moved, pieces):
    count, seg = pieces[0].shape[1:]
    width = 8 * count
    return pl.pallas_call(
        early_kernel,
        in_specs=[pl.BlockSpec(memory_space=pltpu.SMEM)] + [INSIDE] * 9,
        out_specs=[INSIDE] * 2,
        out_shape=[
            jax.ShapeDtypeStruct((LAGS, count, width), jnp.float32),
            jax.ShapeDtypeStruct((8, width), jnp.float32),
        ],
        scratch_shapes=[pltpu.VMEM((width, PAIR * seg), jnp.bfloat16)],
        compiler_params=pltpu.CompilerParams(vmem_limit_bytes=32 * 2**20),
        cost_estimate=pl.CostEstimate(
            flops=2 * LAGS * count * width * PAIR * seg, bytes_accessed=0, transcendentals=0
        ),
    )(me, moved, *pieces)


def late_kernel(me, moved, row_scale, before, energy, *refs):
    pieces, (out, columns, col_scale) = refs[:8], refs[8:]
    group = pl.program_id(0)

    @pl.when(group == 0)
    def _():
        total = energy[...] + place_columns(me[0], pieces, columns)
        col_scale[...] = lax.rsqrt(total / (PAIR * columns.shape[1]) + 1e-06)

    products = group_products(moved, columns, PAIR, group)
    products += before[pl.ds(group * GROUP, GROUP)]
    scaled = products * row_scale[:, :1][None] * col_scale[:1][None]
    out[...] = scaled.astype(jnp.bfloat16)


def match_late(me, moved, row_scale, before, energy, pieces):
    count, seg = pieces[0].shape[1:]
    width = 8 * count
    return pl.pallas_call(
        late_kernel,
        grid=(LAGS // GROUP,),
        in_specs=[pl.BlockSpec(memory_space=pltpu.SMEM)] + [INSIDE] * 12,
        out_specs=pl.BlockSpec((GROUP, count, width), lambda g: (g, 0, 0)),
        out_shape=jax.ShapeDtypeStruct((LAGS, count, width), jnp.bfloat16),
        scratch_shapes=[
            pltpu.VMEM((width, PAIR * seg), jnp.bfloat16),
            pltpu.VMEM((8, width), jnp.float32),
        ],
        compiler_params=pltpu.CompilerParams(vmem_limit_bytes=32 * 2**20),
        cost_estimate=pl.CostEstimate(
            flops=2 * LAGS * count * width * PAIR * seg,
            bytes_accessed=2 * LAGS * count * width,
            transcendentals=0,
        ),
    )(me, moved, row_scale, before, energy, *pieces)


def spread(mine):
    return [mine, send(mine, other_y), send(mine, along_z(-1)), send(mine, along_z(1))]


def swap(pieces):
    return [send(piece, other_core) for piece in pieces]


def on_device(series):
    me = (lax.axis_index("chan") * XS + lax.axis_index("seg")).reshape(1)
    left = send(series, along_x(1))
    right = send(series, along_x(-1))
    far = send(series, along_x(2))
    early, late = whole_window(me, series, left, right, far)
    moved, row_scale = shifts(early, late)
    early = send(early, to_columns)
    late = send(late, to_columns)
    early, moved, row_scale = lax.optimization_barrier((early, moved, row_scale))
    early = spread(early)
    late = spread(late)
    partial, energy = match_early(me, moved, early + swap(early))
    *late, partial, energy = lax.optimization_barrier((*late, partial, energy))
    return match_late(me, moved, row_scale, partial, energy, late + swap(late))


def solution(mesh):
    placed = (P("chan", ("win", "seg")),)
    return jax.shard_map(
        on_device, mesh=mesh, in_specs=placed, out_specs=P("win", "chan", "seg"), check_vma=False
    )
```

```python
import functools
import itertools

import jax
import jax.numpy as jnp
import numpy as np
from jax import lax
from jax.experimental import pallas as pl
from jax.experimental.pallas import tpu as pltpu
from jax.sharding import PartitionSpec as P

HALF_LAG = 32
LAGS = 2 * HALF_LAG + 1
AXES = ("chan", "seg", "win")
ZS, HS, KS, XS, WS = 8, 2, 2, 4, 2
EDGE = 128

PHASES = 4
REACH = HALF_LAG // PHASES
TILES = 2 * (2 * REACH + 1)
BLOCKS = (range(0, 11), range(11, 22), range(22, HALF_LAG + 1))
INSIDE = pl.BlockSpec(memory_space=pltpu.VMEM)
ANYWHERE = pl.BlockSpec(memory_space=pl.ANY)
SCALAR = pl.BlockSpec(memory_space=pltpu.SMEM)

JUMP = ((2, 0, -2, 4), (-2, 4, 2, 0))


def pairs(target):
    places = itertools.product(range(ZS), range(HS), range(KS), range(XS), range(WS))
    shape = (ZS, HS, KS, XS, WS)
    return [
        (int(np.ravel_multi_index(p, shape)), int(np.ravel_multi_index(target(*p), shape)))
        for p in places
    ]


def send(value, target):
    return lax.ppermute(value, AXES, pairs(target))


def along_x(step):
    return lambda z, h, k, x, w: (z, h, k, (x + step) % XS, w)


def other_y(z, h, k, x, w):
    return z, 1 - h, k, x, w


def other_core(z, h, k, x, w):
    return z, h, 1 - k, x, w


def to_columns(z, h, k, x, w):
    jump = JUMP[k][x]
    return (z + jump) % ZS, h if jump % 4 == 0 else 1 - h, k, z // 2, w


def along_z(step):
    return lambda z, h, k, x, w: ((z + step) % ZS, h, k, x, w)


def held(me, step):
    h, z = lax.rem(me // (XS * KS), HS), me // (XS * KS * HS)
    q = (z - 2 * lax.rem(me, XS) + step) & 3
    return q & 1, h ^ (q >> 1)


def own_kernel(series, out, move, rows, sem):
    copy = pltpu.make_async_copy(series, rows, sem)
    copy.start()
    seg = series.shape[1]
    sample = lax.broadcasted_iota(jnp.int32, (seg, seg), 0)
    place = lax.broadcasted_iota(jnp.int32, (seg, seg), 1)
    goes = (sample & (PHASES - 1)) * EDGE + sample // PHASES == place
    move[...] = jnp.where(goes, 1.0, 0.0).astype(jnp.bfloat16)
    copy.wait()
    values = jnp.dot(rows[...], move[...], preferred_element_type=jnp.float32)
    out[...] = values.astype(jnp.bfloat16)


def own_segment(series):
    count, seg = series.shape
    return pl.pallas_call(
        own_kernel,
        in_specs=[ANYWHERE],
        out_specs=[INSIDE] * 2,
        out_shape=[
            jax.ShapeDtypeStruct((count, seg), jnp.bfloat16),
            jax.ShapeDtypeStruct((seg, seg), jnp.bfloat16),
        ],
        scratch_shapes=[pltpu.VMEM((count, seg), jnp.bfloat16), pltpu.SemaphoreType.DMA],
        compiler_params=pltpu.CompilerParams(vmem_limit_bytes=16 * 2**20),
        cost_estimate=pl.CostEstimate(
            flops=2 * count * seg * seg, bytes_accessed=2 * 2**20, transcendentals=0
        ),
    )(series)


def window_kernel(me, own, move, left, right, far, out):
    x = lax.rem(me[0], XS)
    out[pl.ds(x, 1)] = own[...][None]
    for piece, step in ((left, XS - 1), (right, 1), (far, 2)):
        values = jnp.dot(piece[...], move[...], preferred_element_type=jnp.float32)
        out[pl.ds(lax.rem(x + step, XS), 1)] = values.astype(jnp.bfloat16)[None]


def whole_window(me, own, move, left, right, far):
    return pl.pallas_call(
        window_kernel,
        in_specs=[SCALAR] + [INSIDE] * 5,
        out_specs=INSIDE,
        out_shape=jax.ShapeDtypeStruct((XS,) + own.shape, own.dtype),
        compiler_params=pltpu.CompilerParams(vmem_limit_bytes=16 * 2**20),
    )(me, own, move, left, right, far)


def shift_kernel(window, even, odd, both, scale):
    count, seg = window.shape[1:]
    edge = jnp.zeros((count, EDGE), jnp.bfloat16)
    total = jnp.zeros((count, 1), jnp.float32)
    for g in range(XS):
        wide = window[g].astype(jnp.float32)
        total += jnp.sum(wide * wide, axis=1, keepdims=True)
    samples = seg * XS
    norm = lax.rsqrt(total / samples + 1e-06) * (1.0 / np.sqrt(samples))
    scale[...] = jnp.broadcast_to(norm, scale.shape)
    phase = []
    for j in range(PHASES):
        tiles = [window[g, :, j * EDGE : (j + 1) * EDGE] for g in range(XS)]
        phase.append(jnp.concatenate([edge] + tiles + [edge], axis=1))
    wide = [row.astype(jnp.float32) for row in phase]
    sums = [wide[0] + pltpu.roll(wide[3], 1, 1), wide[2] + wide[1]]
    sums = [row.astype(jnp.bfloat16) for row in sums]
    for out, rows in ((even, phase[0::2]), (odd, phase[1::2]), (both, sums)):
        for a, row in enumerate(rows):
            for o in range(2 * REACH + 1):
                moved = pltpu.roll(row, (REACH - o) % row.shape[1], 1)
                at = (2 * o + a) * EDGE
                for g in range(XS):
                    out[g, :, at : at + EDGE] = moved[:, (g + 1) * EDGE : (g + 2) * EDGE]


def shifts(window):
    count = window.shape[1]
    shape = (XS, count, TILES * EDGE)
    return pl.pallas_call(
        shift_kernel,
        in_specs=[INSIDE],
        out_specs=[INSIDE] * 4,
        out_shape=[jax.ShapeDtypeStruct(shape, jnp.bfloat16)] * 3
        + [jax.ShapeDtypeStruct((count, EDGE), jnp.float32)],
        compiler_params=pltpu.CompilerParams(vmem_limit_bytes=16 * 2**20),
        cost_estimate=pl.CostEstimate(
            flops=0, bytes_accessed=6 * int(np.prod(shape)), transcendentals=0
        ),
    )(window)


def match_kernel(step, me, even, odd, both, row_scale, *refs):
    pieces, (out, c_even, c_odd, c_both, done, sems) = refs[:4], refs[-6:]
    count, seg = pieces[0].shape[1:]
    width = c_even.shape[0]
    r, h = held(me[0], step)
    k = lax.rem(me[0] // XS, KS)
    for piece, at in zip(pieces, (h * 2 + k, 2 - h * 2 + k, h * 2 + 1 - k, 3 - h * 2 - k)):
        row = pl.ds(pl.multiple_of(at * count, count), count)
        for g in range(XS):
            for a in range(2):
                lanes = slice((2 * g + a) * EDGE, (2 * g + a + 1) * EDGE)
                c_even[row, lanes] = piece[g, :, 2 * a * EDGE : (2 * a + 1) * EDGE]
                c_odd[row, lanes] = piece[g, :, (2 * a + 1) * EDGE : (2 * a + 2) * EDGE]
    wide_even = c_even[...].astype(jnp.float32)
    wide_odd = c_odd[...].astype(jnp.float32)
    c_both[...] = (wide_even + wide_odd).astype(jnp.bfloat16)
    total = jnp.sum(wide_even * wide_even + wide_odd * wide_odd, axis=1, keepdims=True)
    norm = lax.rsqrt(total / (XS * seg) + 1e-06)
    scale = row_scale[:, :1] * jnp.broadcast_to(norm, (width, EDGE)).T[:1]

    def products(rows, steps, columns):
        tiles = [
            jnp.concatenate(
                [
                    rows[g, :, (HALF_LAG - u) * EDGE : (HALF_LAG - u + 2) * EDGE]
                    for g in range(XS)
                ],
                axis=1,
            )
            for u in steps
        ]
        found = lax.dot_general(
            jnp.concatenate(tiles, axis=0),
            columns[...],
            (((1,), (1,)), ((), ())),
            preferred_element_type=jnp.float32,
        )
        return {u: found[n * count : (n + 1) * count] for n, u in enumerate(steps)}

    b = {}
    copies = []
    lanes = pl.ds(pl.multiple_of(r * width, width), width)
    for n, block in enumerate(BLOCKS):
        a = products(even, block, c_even)
        ahead = range(block[0], min(block[-1] + 2, HALF_LAG + 1))
        b.update(products(odd, [u for u in ahead if u not in b], c_odd))
        s = products(both, [u for u in block if u < HALF_LAG], c_both)
        for u in block:
            done[2 * u] = ((a[u] + b[u]) * scale).astype(jnp.bfloat16)
            if u in s:
                done[2 * u + 1] = ((s[u] - a[u] - b[u + 1]) * scale).astype(jnp.bfloat16)
        lags = pl.ds(2 * block[0], min(2 * len(block), LAGS - 2 * block[0]))
        copy = pltpu.make_async_copy(done.at[lags], out.at[lags, :, lanes], sems.at[n])
        copy.start()
        copies.append(copy)
    for copy in copies:
        copy.wait()


def match(me, step, rows, row_scale, pieces, result, columns):
    count, seg = pieces[0].shape[1:]
    samples = seg * XS
    width = 4 * count
    before = [] if result is None else [result]
    return pl.pallas_call(
        functools.partial(match_kernel, step),
        in_specs=[SCALAR] + [INSIDE] * 8 + [ANYWHERE] * len(before),
        out_specs=ANYWHERE,
        out_shape=jax.ShapeDtypeStruct((LAGS, count, columns), jnp.bfloat16),
        scratch_shapes=[pltpu.VMEM((width, samples // 2), jnp.bfloat16)] * 3
        + [
            pltpu.VMEM((LAGS, count, width), jnp.bfloat16),
            pltpu.SemaphoreType.DMA((len(BLOCKS),)),
        ],
        input_output_aliases={9: 0} if before else {},
        compiler_params=pltpu.CompilerParams(vmem_limit_bytes=24 * 2**20),
        cost_estimate=pl.CostEstimate(
            flops=3 * (LAGS + 1) * count * width * samples // 2,
            bytes_accessed=2 * LAGS * count * width,
            transcendentals=0,
        ),
    )(me, *rows, row_scale, *pieces, *before)


def on_device(series):
    count = series.shape[0]
    me = (lax.axis_index("chan") * XS + lax.axis_index("seg")).reshape(1)
    left = send(series, along_x(1))
    right = send(series, along_x(-1))
    far = send(series, along_x(2))
    own, move = own_segment(series)
    window = whole_window(me, own, move, left, right, far)
    *rows, row_scale = shifts(window)
    mine = send(window, to_columns)
    mine, row_scale, *rows = lax.optimization_barrier((mine, row_scale, *rows))
    beside = send(mine, other_y)
    above = send(mine, along_z(-1))
    below = send(mine, along_z(1))
    result = None
    for step, (first, second) in enumerate(((mine, beside), (above, below))):
        pieces = (first, second, send(first, other_core), send(second, other_core))
        result = match(me, step, rows, row_scale, pieces, result, 8 * count)
    return result


def solution(mesh):
    placed = (P("chan", ("win", "seg")),)
    return jax.shard_map(
        on_device, mesh=mesh, in_specs=placed, out_specs=P("win", "chan", "seg"), check_vma=False
    )
```

```python
import functools
import itertools

import jax
import jax.numpy as jnp
import numpy as np
from jax import lax
from jax.experimental import pallas as pl
from jax.experimental.pallas import tpu as pltpu
from jax.sharding import PartitionSpec as P

HALF_LAG = 32
LAGS = 2 * HALF_LAG + 1
AXES = ("chan", "seg", "win")
ZS, HS, KS, XS, WS = 8, 2, 2, 4, 2
EDGE = 128

PHASES = 4
REACH = HALF_LAG // PHASES
TILES = 2 * (2 * REACH + 1)
BLOCKS = (range(0, 13), range(13, 26), range(26, HALF_LAG + 1))
INSIDE = pl.BlockSpec(memory_space=pltpu.VMEM)
ANYWHERE = pl.BlockSpec(memory_space=pl.ANY)
SCALAR = pl.BlockSpec(memory_space=pltpu.SMEM)

JUMP = ((2, 0, -2, 4), (-2, 4, 2, 0))


def pairs(target):
    places = itertools.product(range(ZS), range(HS), range(KS), range(XS), range(WS))
    shape = (ZS, HS, KS, XS, WS)
    return [
        (int(np.ravel_multi_index(p, shape)), int(np.ravel_multi_index(target(*p), shape)))
        for p in places
    ]


def send(value, target):
    return lax.ppermute(value, AXES, pairs(target))


def along_x(step):
    return lambda z, h, k, x, w: (z, h, k, (x + step) % XS, w)


def other_y(z, h, k, x, w):
    return z, 1 - h, k, x, w


def other_core(z, h, k, x, w):
    return z, h, 1 - k, x, w


def to_columns(z, h, k, x, w):
    jump = JUMP[k][x]
    return (z + jump) % ZS, h if jump % 4 == 0 else 1 - h, k, z // 2, w


def along_z(step):
    return lambda z, h, k, x, w: ((z + step) % ZS, h, k, x, w)


def held(me, step):
    h, z = lax.rem(me // (XS * KS), HS), me // (XS * KS * HS)
    q = (z - 2 * lax.rem(me, XS) + step) & 3
    return q & 1, h ^ (q >> 1)


def own_kernel(series, out, move, rows, sem):
    copy = pltpu.make_async_copy(series, rows, sem)
    copy.start()
    seg = series.shape[1]
    sample = lax.broadcasted_iota(jnp.int32, (seg, seg), 0)
    place = lax.broadcasted_iota(jnp.int32, (seg, seg), 1)
    goes = (sample & (PHASES - 1)) * EDGE + sample // PHASES == place
    move[...] = jnp.where(goes, 1.0, 0.0).astype(jnp.bfloat16)
    copy.wait()
    values = jnp.dot(rows[...], move[...], preferred_element_type=jnp.float32)
    out[...] = values.astype(jnp.bfloat16)


def own_segment(series):
    count, seg = series.shape
    return pl.pallas_call(
        own_kernel,
        in_specs=[ANYWHERE],
        out_specs=[INSIDE] * 2,
        out_shape=[
            jax.ShapeDtypeStruct((count, seg), jnp.bfloat16),
            jax.ShapeDtypeStruct((seg, seg), jnp.bfloat16),
        ],
        scratch_shapes=[pltpu.VMEM((count, seg), jnp.bfloat16), pltpu.SemaphoreType.DMA],
        compiler_params=pltpu.CompilerParams(vmem_limit_bytes=16 * 2**20),
        cost_estimate=pl.CostEstimate(
            flops=2 * count * seg * seg, bytes_accessed=2 * 2**20, transcendentals=0
        ),
    )(series)


def window_kernel(me, own, move, left, right, far, out):
    x = lax.rem(me[0], XS)
    out[pl.ds(x, 1)] = own[...][None]
    for piece, step in ((left, XS - 1), (right, 1), (far, 2)):
        values = jnp.dot(piece[...], move[...], preferred_element_type=jnp.float32)
        out[pl.ds(lax.rem(x + step, XS), 1)] = values.astype(jnp.bfloat16)[None]


def whole_window(me, own, move, left, right, far):
    return pl.pallas_call(
        window_kernel,
        in_specs=[SCALAR] + [INSIDE] * 5,
        out_specs=INSIDE,
        out_shape=jax.ShapeDtypeStruct((XS,) + own.shape, own.dtype),
        compiler_params=pltpu.CompilerParams(vmem_limit_bytes=16 * 2**20),
    )(me, own, move, left, right, far)


def shift_kernel(window, even, odd, both, scale):
    count, seg = window.shape[1:]
    edge = jnp.zeros((count, EDGE), jnp.bfloat16)
    total = jnp.zeros((count, 1), jnp.float32)
    for g in range(XS):
        wide = window[g].astype(jnp.float32)
        total += jnp.sum(wide * wide, axis=1, keepdims=True)
    samples = seg * XS
    norm = lax.rsqrt(total / samples + 1e-06) * (1.0 / np.sqrt(samples))
    scale[...] = jnp.broadcast_to(norm, scale.shape)
    phase = []
    for j in range(PHASES):
        tiles = [window[g, :, j * EDGE : (j + 1) * EDGE] for g in range(XS)]
        phase.append(jnp.concatenate([edge] + tiles + [edge], axis=1))
    wide = [row.astype(jnp.float32) for row in phase]
    sums = [wide[0] + pltpu.roll(wide[3], 1, 1), wide[2] + wide[1]]
    sums = [row.astype(jnp.bfloat16) for row in sums]
    for out, rows in ((even, phase[0::2]), (odd, phase[1::2]), (both, sums)):
        for a, row in enumerate(rows):
            for o in range(2 * REACH + 1):
                moved = pltpu.roll(row, (REACH - o) % row.shape[1], 1)
                at = (2 * o + a) * EDGE
                for g in range(XS):
                    out[g, :, at : at + EDGE] = moved[:, (g + 1) * EDGE : (g + 2) * EDGE]


def shifts(window):
    count = window.shape[1]
    shape = (XS, count, TILES * EDGE)
    return pl.pallas_call(
        shift_kernel,
        in_specs=[INSIDE],
        out_specs=[INSIDE] * 4,
        out_shape=[jax.ShapeDtypeStruct(shape, jnp.bfloat16)] * 3
        + [jax.ShapeDtypeStruct((count, EDGE), jnp.float32)],
        compiler_params=pltpu.CompilerParams(vmem_limit_bytes=16 * 2**20),
        cost_estimate=pl.CostEstimate(
            flops=0, bytes_accessed=6 * int(np.prod(shape)), transcendentals=0
        ),
    )(window)


def match_kernel(step, me, even, odd, both, row_scale, *refs):
    pieces, (out, c_even, c_odd, c_both, done, sems) = refs[:4], refs[-6:]
    count, seg = pieces[0].shape[1:]
    width = c_even.shape[0]
    r, h = held(me[0], step)
    k = lax.rem(me[0] // XS, KS)
    for piece, at in zip(pieces, (h * 2 + k, 2 - h * 2 + k, h * 2 + 1 - k, 3 - h * 2 - k)):
        row = pl.ds(pl.multiple_of(at * count, count), count)
        for g in range(XS):
            for a in range(2):
                lanes = slice((2 * g + a) * EDGE, (2 * g + a + 1) * EDGE)
                c_even[row, lanes] = piece[g, :, 2 * a * EDGE : (2 * a + 1) * EDGE]
                c_odd[row, lanes] = piece[g, :, (2 * a + 1) * EDGE : (2 * a + 2) * EDGE]
    wide_even = c_even[...].astype(jnp.float32)
    wide_odd = c_odd[...].astype(jnp.float32)
    c_both[...] = (wide_even + wide_odd).astype(jnp.bfloat16)
    total = jnp.sum(wide_even * wide_even + wide_odd * wide_odd, axis=1, keepdims=True)
    norm = lax.rsqrt(total / (XS * seg) + 1e-06)
    scale = row_scale[:, :1] * jnp.broadcast_to(norm, (width, EDGE)).T[:1]

    def products(rows, steps, columns):
        tiles = [
            jnp.concatenate(
                [
                    rows[g, :, (HALF_LAG - u) * EDGE : (HALF_LAG - u + 2) * EDGE]
                    for g in range(XS)
                ],
                axis=1,
            )
            for u in steps
        ]
        found = lax.dot_general(
            jnp.concatenate(tiles, axis=0),
            columns[...],
            (((1,), (1,)), ((), ())),
            preferred_element_type=jnp.float32,
        )
        return {u: found[n * count : (n + 1) * count] for n, u in enumerate(steps)}

    b = {}
    copies = []
    lanes = pl.ds(pl.multiple_of(r * width, width), width)
    for n, block in enumerate(BLOCKS):
        a = products(even, block, c_even)
        ahead = range(block[0], min(block[-1] + 2, HALF_LAG + 1))
        b.update(products(odd, [u for u in ahead if u not in b], c_odd))
        s = products(both, [u for u in block if u < HALF_LAG], c_both)
        for u in block:
            done[2 * u] = ((a[u] + b[u]) * scale).astype(jnp.bfloat16)
            if u in s:
                done[2 * u + 1] = ((s[u] - a[u] - b[u + 1]) * scale).astype(jnp.bfloat16)
        lags = pl.ds(2 * block[0], min(2 * len(block), LAGS - 2 * block[0]))
        copy = pltpu.make_async_copy(done.at[lags], out.at[lags, :, lanes], sems.at[n])
        copy.start()
        copies.append(copy)
    for copy in copies:
        copy.wait()


def match(me, step, rows, row_scale, pieces, result, columns):
    count, seg = pieces[0].shape[1:]
    samples = seg * XS
    width = 4 * count
    before = [] if result is None else [result]
    return pl.pallas_call(
        functools.partial(match_kernel, step),
        in_specs=[SCALAR] + [INSIDE] * 8 + [ANYWHERE] * len(before),
        out_specs=ANYWHERE,
        out_shape=jax.ShapeDtypeStruct((LAGS, count, columns), jnp.bfloat16),
        scratch_shapes=[pltpu.VMEM((width, samples // 2), jnp.bfloat16)] * 3
        + [
            pltpu.VMEM((LAGS, count, width), jnp.bfloat16),
            pltpu.SemaphoreType.DMA((len(BLOCKS),)),
        ],
        input_output_aliases={9: 0} if before else {},
        compiler_params=pltpu.CompilerParams(vmem_limit_bytes=24 * 2**20),
        cost_estimate=pl.CostEstimate(
            flops=3 * (LAGS + 1) * count * width * samples // 2,
            bytes_accessed=2 * LAGS * count * width,
            transcendentals=0,
        ),
    )(me, *rows, row_scale, *pieces, *before)


def on_device(series):
    count = series.shape[0]
    me = (lax.axis_index("chan") * XS + lax.axis_index("seg")).reshape(1)
    left = send(series, along_x(1))
    right = send(series, along_x(-1))
    far = send(series, along_x(2))
    own, move = own_segment(series)
    window = whole_window(me, own, move, left, right, far)
    *rows, row_scale = shifts(window)
    mine = send(window, to_columns)
    mine, row_scale, *rows = lax.optimization_barrier((mine, row_scale, *rows))
    beside = send(mine, other_y)
    above = send(mine, along_z(-1))
    below = send(mine, along_z(1))
    result = None
    for step, (first, second) in enumerate(((mine, beside), (above, below))):
        first, second = lax.optimization_barrier((first, second))
        pieces = (first, second, send(first, other_core), send(second, other_core))
        result = match(me, step, rows, row_scale, pieces, result, 8 * count)
    return result


def solution(mesh):
    placed = (P("chan", ("win", "seg")),)
    return jax.shard_map(
        on_device, mesh=mesh, in_specs=placed, out_specs=P("win", "chan", "seg"), check_vma=False
    )
```
